512 devices in a mesh: row: 128 (over y, z, core), col: 4 (over x).
Axes of the slice: x: 4, y: 4, z: 16, core: 2. Of those that a mesh axis runs over, the one named last changes fastest.
Arguments:
- blocks: bfloat16 [1024, 5, 256, 256], P('row', None, 'col'), may hold values from -0.15625 to 0.15625
- samples: bfloat16 [1024, 256, 256], P('row', 'col'), may hold values from -6 to 6
- probes: bfloat16 [1024, 256, 256], P('row', 'col'), may hold values from -6 to 6
- compress: float32 [256, 128], replicated, may hold values from -0.375 to 0.375
- pattern: int32 [1024, 5], P('row'), may hold values from -8 to 1031, as said below
- ranks: int32 [6], replicated, may hold values from 32 to 128
Outputs:
- leaf_bases: bfloat16 [2, 1024, 256, 128], P(None, ('row', 'col'))
- transfers: bfloat16 [2, 512, 5, 256, 128], P(None, ('row', 'col'))
The draws below stay inside these ranges and needn't reach their ends.
Inputs may be any that keep to these rules, and one draw needn't show every extreme that they name: `pattern`: block row i names column blocks i - 8, i - o, i, i + p, i + 8 in that order, with o and p from 1 to 7.
All inputs are finite; a program needn't handle non-finite values.
Results may differ from the reference program's by a relative error of at most 0.001.
Values may be sent and summed in bfloat16 or wider, within the bound.
A program may use at most 64 MiB of HBM per device.

```python
import math
import jax
import jax.numpy as jnp
from jax import lax

B = 256
S = 256
K = 128
NNZ = 5
LPD = 2
CROSS = 5
RANKS = 6
BPD = 8
BLOCKS = 1024


def draw_pattern(key, part):
    key = jax.random.fold_in(key, 11)
    first, second = jax.random.split(key)
    rows = jnp.arange(BLOCKS, dtype=jnp.int32)
    back = jax.random.randint(first, (BLOCKS,), 1, BPD, dtype=jnp.int32)
    ahead = jax.random.randint(second, (BLOCKS,), 1, BPD, dtype=jnp.int32)
    return jnp.stack([rows - BPD, rows - back, rows, rows + ahead, rows + BPD], axis=1).astype(jnp.int32)


def draw_ranks(key, part):
    key = jax.random.fold_in(key, 23)
    first, second = jax.random.split(key)
    values = jax.random.randint(first, (RANKS,), K // 4, K + 1, dtype=jnp.int32)
    order = jax.random.permutation(second, RANKS)
    values = values.at[order[0]].set(K)
    values = values.at[order[1]].set(K // 4)
    return values.astype(jnp.int32)


def block_scale(key, extent, cuts, low, top_value):
    level = 1.0
    for position, parts in cuts:
        steps = jax.random.uniform(jax.random.fold_in(jax.random.fold_in(key, 6), position), (parts,), jnp.float32, low / len(cuts), top_value / len(cuts))
        level = level * jnp.repeat(jnp.exp(steps), extent[position] // parts).reshape((-1,) + (1,) * (len(extent) - 1 - position))
    return level


def bell_draw(rng, dims, width, most, shards=(), kind=jnp.bfloat16):
    result = jax.random.normal(rng, dims, jnp.float32) * width
    if len(shards) > 0:
        result = block_scale(rng, dims, shards, -0.22, 0.18) * result
    return jnp.clip(result, min=-most, max=most).astype(kind)


def setup_inputs(seed: int = 0) -> dict:
    streams_of = jax.random.split(jax.random.key(seed), 7)
    return {
        "blocks": bell_draw(streams_of[0], (BLOCKS, NNZ, B, B), (NNZ * B) ** -0.5, 0.15625, ((0, 128), (2, 4))),
        "samples": bell_draw(streams_of[1], (BLOCKS, B, S), 1.0, 6.0, ((0, 128), (1, 4))),
        "probes": bell_draw(streams_of[2], (BLOCKS, B, S), 1.0, 6.0, ((0, 128), (1, 4))),
        "compress": bell_draw(streams_of[3], (S, K), S ** -0.5, 0.375, (), jnp.float32),
        "pattern": draw_pattern(jax.random.fold_in(streams_of[6], 71), 0),
        "ranks": draw_ranks(jax.random.fold_in(streams_of[6], 71), 0),
    }


def leaf_factor(sketch, compress):
    hp = lax.Precision.HIGHEST
    wide = jnp.einsum('...bs,sk->...bk', sketch, compress, precision=hp)
    gram = jnp.einsum('...bk,...bj->...kj', wide, wide, precision=hp)
    factor = jnp.linalg.cholesky(gram)
    unit = lax.linalg.triangular_solve(factor, wide, left_side=False, lower=True, transpose_a=True)
    return (factor, unit)

def combine(lower_node, upper_node):
    hp = lax.Precision.HIGHEST
    stacked = jnp.concatenate([jnp.swapaxes(lower_node, -1, -2), jnp.swapaxes(upper_node, -1, -2)], axis=-2)
    gram = jnp.einsum('...ik,...jk->...ij', lower_node, lower_node, precision=hp)
    gram = gram + jnp.einsum('...ik,...jk->...ij', upper_node, upper_node, precision=hp)
    factor = jnp.linalg.cholesky(gram)
    basis = lax.linalg.triangular_solve(factor, stacked, left_side=False, lower=True, transpose_a=True)
    return (factor, basis)

def reference(blocks, samples, probes, compress, pattern, ranks):
    hp = lax.Precision.HIGHEST
    padded = jnp.pad(samples, ((BPD, BPD), (0, 0), (0, 0)))
    index = (pattern + BPD).astype(jnp.int32)
    groups = BLOCKS // LPD

    def row_group(g):
        start = (g * LPD).astype(jnp.int32)
        part = lax.dynamic_slice_in_dim(blocks, start, LPD, 0).astype(jnp.float32)
        where = lax.dynamic_slice_in_dim(index, start, LPD, 0)
        picked = padded[where].astype(jnp.float32)
        return jnp.einsum('nkrc,nkcs->nrs', part, picked, precision=hp)
    row_sketch = lax.map(row_group, jnp.arange(groups, dtype=jnp.int32)).reshape(BLOCKS, B, S)

    def add_group(total, g):
        start = (g * LPD).astype(jnp.int32)
        part = lax.dynamic_slice_in_dim(blocks, start, LPD, 0).astype(jnp.float32)
        where = lax.dynamic_slice_in_dim(index, start, LPD, 0)
        probe = lax.dynamic_slice_in_dim(probes, start, LPD, 0).astype(jnp.float32)
        terms = jnp.einsum('nkrc,nrs->nkcs', part, probe, precision=hp)
        total = total.at[where.reshape(-1)].add(terms.reshape(-1, B, S))
        return (total, None)
    total = jnp.zeros((BLOCKS + 2 * BPD, B, S), jnp.float32)
    total, unused = lax.scan(add_group, total, jnp.arange(groups, dtype=jnp.int32))
    col_sketch = total[BPD:BPD + BLOCKS]
    sides = jnp.stack([row_sketch, col_sketch])
    factor, unit = leaf_factor(sides, compress)
    columns = jnp.arange(K, dtype=jnp.int32)
    leaf_mask = (columns < ranks[0]).astype(jnp.float32)
    leaf_bases = (unit * math.sqrt(B) * leaf_mask).astype(jnp.bfloat16)
    local_levels = LPD.bit_length() - 1
    collected = []
    current = factor
    for level in range(1, local_levels + CROSS + 1):
        count = current.shape[1] // 2
        paired = current.reshape(2, count, 2, K, K)
        current, basis = combine(paired[:, :, 0], paired[:, :, 1])
        if level > local_levels:
            step = level - local_levels - 1
            mask = (columns < ranks[step + 1]).astype(jnp.float32)
            scaled = basis * math.sqrt(2 * K) * mask
            collected.append(jnp.repeat(scaled, 2 ** (step + 1), axis=1))
    transfers = jnp.stack(collected, axis=2).astype(jnp.bfloat16)
    return (leaf_bases, transfers)
```

```python
import math

import jax
import jax.numpy as jnp
from jax import lax
from jax.experimental import pallas as pl
from jax.experimental.pallas import tpu as pltpu
from jax.sharding import PartitionSpec as P

ROW_LEVELS = 3


def padded(value, sides, width):
    for axis, dim in sides:
        size, length = (lax.axis_size(axis), value.shape[dim])
        up = [(i, (i + 1) % size) for i in range(size - 1)]
        down = [(j, i) for i, j in up]
        last = lax.slice_in_dim(value, length - width, length, axis=dim)
        initial = lax.slice_in_dim(value, 0, width, axis=dim)
        before = lax.ppermute(last, axis, up)
        after = lax.ppermute(initial, axis, down)
        value = jnp.concatenate([before, value, after], axis=dim)
    return value


def passed_along(value, axis, by):
    size = lax.axis_size(axis)
    pairs = [(i, i + by) for i in range(size) if 0 <= i + by < size]
    return lax.ppermute(value, axis, pairs)


def partner(value, axis, distance):
    return lax.ppermute(value, axis, [(i, i ^ 1 << distance) for i in range(lax.axis_size(axis))])


K = 128
F32 = jnp.float32
BF16 = jnp.bfloat16

def pieces(x):
    h = x.astype(BF16).astype(F32)
    r = x - h
    m = r.astype(BF16).astype(F32)
    return h, m, r - m

def panel(S, E, g, p, with_e):
    base = (g * 16 + p) * 64
    rows = [S[pl.ds(base + r, 8, stride=8), :] for r in range(8)]
    erows = [E[pl.ds(base + r, 8, stride=8), :] for r in range(8)] if with_e else None
    a = {}
    for r in range(8):
        for k in range(r, 8):
            c = 8 * p + k
            a[r, k] = jnp.broadcast_to(rows[r][:, c:c + 1], (8, K))
    for r in range(8):
        inv = lax.rsqrt(a[r, r])
        u = {k: a[r, k] * inv for k in range(r + 1, 8)}
        rows[r] = rows[r] * inv
        if with_e:
            erows[r] = erows[r] * inv
        for i in range(r + 1, 8):
            for k in range(i, 8):
                a[i, k] = a[i, k] - u[i] * u[k]
            rows[i] = rows[i] - u[i] * rows[r]
            if with_e:
                erows[i] = erows[i] - u[i] * erows[r]
    for r in range(8):
        S[pl.ds(base + r, 8, stride=8), :] = rows[r]
        if with_e:
            E[pl.ds(base + r, 8, stride=8), :] = erows[r]

def trail(S, E, g, p, b, with_e):
    if p == 15:
        return
    at = lambda q: pl.ds(((g * 16 + q) * 8 + b) * 8, 8)
    h, m, l = pieces(S[at(p), :])
    first = (8 * (p + 1)) // 16 * 16
    left = jnp.concatenate([h, h, h, m, m, l], axis=0).T[first:].astype(BF16)
    right = jnp.concatenate([h, m, l, h, m, h], axis=0)
    if with_e:
        h, m, l = pieces(E[at(p), :])
        right = jnp.concatenate([right, jnp.concatenate([h, m, l, h, m, h], axis=0)], axis=1)
    t = jnp.dot(left, right.astype(BF16), preferred_element_type=F32)
    for q in range(p + 1, 16):
        o = 8 * q - first
        S[at(q), :] = S[at(q), :] - t[o:o + 8, :K]
        if with_e:
            E[at(q), :] = E[at(q), :] - t[o:o + 8, K:]

def get(ref, g, b):
    return jnp.concatenate([ref[pl.ds(((g * 16 + q) * 8 + b) * 8, 8), :] for q in range(16)], axis=0)

def put(ref, g, b, x):
    for q in range(16):
        ref[pl.ds(((g * 16 + q) * 8 + b) * 8, 8), :] = x[8 * q:8 * q + 8]

def cat(x, order):
    h, m, l = x
    d = {"h": h, "m": m, "l": l}
    return jnp.concatenate([d[c] for c in order], axis=1)

def exact_nt(x, y):
    a = cat([v.astype(BF16) for v in pieces(x)], "hhmhml")
    b = cat([v.astype(BF16) for v in pieces(y)], "hmhlmh")
    return lax.dot_general(a, b, (((1,), (1,)), ((), ())), preferred_element_type=F32)

def kernel(bits, ranks, wide, gram, own1, chain, sib, leaf_out, tr_out, S, E):
    eye = (lax.broadcasted_iota(jnp.int32, (K, K), 0) == lax.broadcasted_iota(jnp.int32, (K, K), 1)).astype(F32)
    def place(i, x):
        put(S, i // 8, i % 8, x)
    for s in range(2):
        for l in range(2):
            place(s * 2 + l, gram[s, l])
        for j in range(5):
            place(4 + s * 5 + j, chain[s, j])
            place(18 + s * 5 + j, sib[s, j])
        place(16 + s, own1[s])
    for i in (14, 15, 28, 29, 30, 31):
        place(i, eye)
    for g in range(2):
        for b in range(8):
            put(E, g, b, eye)
    for p in range(16):
        for g in range(4):
            panel(S, E, g, p, g < 2)
        for g in range(4):
            for b in range(8):
                if g * 8 + b in (14, 15, 28, 29, 30, 31):
                    continue
                trail(S, E, g, p, b, g < 2)
    lane = lax.broadcasted_iota(jnp.int32, (K, K), 1)
    X = lambda i: get(E, i // 8, i % 8)
    U = lambda i: jnp.where(lax.broadcasted_iota(jnp.int32, (K, K), 0) <= lane, get(S, i // 8, i % 8), 0.0)
    scale = math.sqrt(256)
    for s in range(2):
        keep = jnp.where(lane < ranks[0], scale, 0.0)
        for l in range(2):
            x = X(s * 2 + l)
            for half in range(2):
                leaf_out[s, l, pl.ds(half * K, K), :] = (exact_nt(wide[s, l, half * K:half * K + K, :], x) * keep).astype(BF16)
        for j in range(5):
            keep = jnp.where(lane < ranks[j + 1], scale, 0.0)
            own = U(16 + s) if j == 0 else U(4 + s * 5 + j - 1)
            other = U(18 + s * 5 + j)
            x = X(4 + s * 5 + j)
            up = bits[j]
            tr_out[s, 0, j, pl.ds(pl.multiple_of(up * K, K), K), :] = (exact_nt(own, x) * keep).astype(BF16)
            tr_out[s, 0, j, pl.ds(pl.multiple_of((1 - up) * K, K), K), :] = (exact_nt(other, x) * keep).astype(BF16)

def finish(bits, ranks, wide, gram, own1, chain, sib):
    vm = pl.BlockSpec(memory_space=pltpu.VMEM)
    sm = pl.BlockSpec(memory_space=pltpu.SMEM)
    return pl.pallas_call(
        kernel,
        out_shape=(jax.ShapeDtypeStruct((2, 2, 256, K), BF16), jax.ShapeDtypeStruct((2, 1, 5, 256, K), BF16)),
        in_specs=[sm, sm, vm, vm, vm, vm, vm],
        out_specs=(vm, vm),
        scratch_shapes=[pltpu.VMEM((4 * 1024, K), F32), pltpu.VMEM((2 * 1024, K), F32)],
        compiler_params=pltpu.CompilerParams(vmem_limit_bytes=48 << 20),
    )(bits, ranks, wide, gram, own1, chain, sib)


def body(blocks, samples, probes, compress, pattern, ranks):
    row_index = lax.axis_index("row")
    col_index = lax.axis_index("col")
    n_blocks = blocks.shape[0]
    n_slots = blocks.shape[1]
    rows_block = blocks.shape[3]
    n_samples = samples.shape[2]
    rank_max = compress.shape[1]
    local_index = pattern - row_index * n_blocks + n_blocks
    full_rows = lax.all_gather(samples, "col", axis=1, tiled=True)
    extended = padded(full_rows, (("row", 0),), n_blocks)
    partial_value = jnp.zeros((n_blocks, blocks.shape[2], n_samples), jnp.float32)
    for slot in range(n_slots):
        picked = extended[local_index[:, slot]]
        partial_value = partial_value + jnp.einsum(
            "nrc,ncs->nrs", blocks[:, slot], picked, preferred_element_type=jnp.float32
        )
    row_sketch = lax.all_to_all(partial_value, "col", split_axis=0, concat_axis=1, tiled=True)
    buffer = jnp.zeros((3 * n_blocks, rows_block, n_samples), jnp.float32)
    for slot in range(n_slots):
        term = jnp.einsum(
            "nrc,nrs->ncs", blocks[:, slot], probes, preferred_element_type=jnp.float32
        )
        buffer = buffer.at[local_index[:, slot]].add(term)
    from_above = passed_along(buffer[:n_blocks], "row", -1)
    from_below = passed_along(buffer[2 * n_blocks :], "row", 1)
    adjoint_part = buffer[n_blocks : 2 * n_blocks] + from_above + from_below
    col_sketch = lax.psum_scatter(adjoint_part, "col", scatter_dimension=0, tiled=True)
    hp = lax.Precision.HIGHEST
    sides = jnp.stack([row_sketch, col_sketch])
    wide = jnp.einsum("...bs,sk->...bk", sides, compress, precision=hp)
    gram = jnp.einsum("...bk,...bj->...kj", wide, wide, precision=hp)
    current = gram[:, 0] + gram[:, 1]
    chain = [current]
    siblings = []
    bits = []
    for axis, index, levels in (("col", col_index, 2), ("row", row_index, ROW_LEVELS)):
        for bit in range(levels):
            other = partner(current, axis, bit)
            current = current + other
            siblings.append(other)
            chain.append(current)
            bits.append(index >> bit & 1)
    return finish(
        jnp.stack(bits), ranks, wide, gram, chain[0], jnp.stack(chain[1:], 1), jnp.stack(siblings, 1)
    )


def solution(mesh):
    return jax.shard_map(
        body,
        mesh=mesh,
        in_specs=(
            P("row", None, "col", None),
            P("row", "col", None),
            P("row", "col", None),
            P(),
            P("row", None),
            P(),
        ),
        out_specs=(P(None, ("row", "col"), None, None), P(None, ("row", "col"), None, None, None)),
        check_vma=False,
    )
```

```python
import math

import jax
import jax.numpy as jnp
from jax import lax
from jax.experimental import pallas as pl
from jax.experimental.pallas import tpu as pltpu
from jax.sharding import PartitionSpec as P

K = 128
F32 = jnp.float32
BF16 = jnp.bfloat16

def pieces(x):
    h = x.astype(BF16).astype(F32)
    r = x - h
    m = r.astype(BF16).astype(F32)
    return h, m, r - m

def panel(S, E, g, p, with_e):
    base = (g * 16 + p) * 64
    rows = [S[pl.ds(base + r, 8, stride=8), :] for r in range(8)]
    erows = [E[pl.ds(base + r, 8, stride=8), :] for r in range(8)] if with_e else None
    a = {}
    for r in range(8):
        for k in range(r, 8):
            c = 8 * p + k
            a[r, k] = jnp.broadcast_to(rows[r][:, c:c + 1], (8, K))
    for r in range(8):
        inv = lax.rsqrt(a[r, r])
        u = {k: a[r, k] * inv for k in range(r + 1, 8)}
        rows[r] = rows[r] * inv
        if with_e:
            erows[r] = erows[r] * inv
        for i in range(r + 1, 8):
            for k in range(i, 8):
                a[i, k] = a[i, k] - u[i] * u[k]
            rows[i] = rows[i] - u[i] * rows[r]
            if with_e:
                erows[i] = erows[i] - u[i] * erows[r]
    for r in range(8):
        S[pl.ds(base + r, 8, stride=8), :] = rows[r]
        if with_e:
            E[pl.ds(base + r, 8, stride=8), :] = erows[r]

def trail(S, E, g, p, b, with_e):
    if p == 15:
        return
    at = lambda q: pl.ds(((g * 16 + q) * 8 + b) * 8, 8)
    h, m, l = pieces(S[at(p), :])
    first = (8 * (p + 1)) // 16 * 16
    left = jnp.concatenate([h, h, h, m, m, l], axis=0).T[first:].astype(BF16)
    right = jnp.concatenate([h, m, l, h, m, h], axis=0)
    if with_e:
        h, m, l = pieces(E[at(p), :])
        right = jnp.concatenate([right, jnp.concatenate([h, m, l, h, m, h], axis=0)], axis=1)
    t = jnp.dot(left, right.astype(BF16), preferred_element_type=F32)
    for q in range(p + 1, 16):
        o = 8 * q - first
        S[at(q), :] = S[at(q), :] - t[o:o + 8, :K]
        if with_e:
            E[at(q), :] = E[at(q), :] - t[o:o + 8, K:]

def get(ref, g, b):
    return jnp.concatenate([ref[pl.ds(((g * 16 + q) * 8 + b) * 8, 8), :] for q in range(16)], axis=0)

def put(ref, g, b, x):
    for q in range(16):
        ref[pl.ds(((g * 16 + q) * 8 + b) * 8, 8), :] = x[8 * q:8 * q + 8]

def cat(x, order):
    h, m, l = x
    d = {"h": h, "m": m, "l": l}
    return jnp.concatenate([d[c] for c in order], axis=1)

def exact_nt(x, y):
    a = cat([v.astype(BF16) for v in pieces(x)], "hhmhml")
    b = cat([v.astype(BF16) for v in pieces(y)], "hmhlmh")
    return lax.dot_general(a, b, (((1,), (1,)), ((), ())), preferred_element_type=F32)

def kernel(bits, ranks, wide, gram, chain, sib, leaf_out, tr_out, S, E):
    eye = (lax.broadcasted_iota(jnp.int32, (K, K), 0) == lax.broadcasted_iota(jnp.int32, (K, K), 1)).astype(F32)
    def place(i, x):
        put(S, i // 8, i % 8, x)
    for s in range(2):
        for l in range(2):
            place(s * 2 + l, gram[s, l])
        for j in range(5):
            place(4 + s * 5 + j, chain[j + 1, s])
            place(18 + s * 5 + j, sib[j, s])
        place(16 + s, chain[0, s])
    for i in (14, 15, 28, 29, 30, 31):
        place(i, eye)
    for g in range(2):
        for b in range(8):
            put(E, g, b, eye)
    for p in range(16):
        for g in range(4):
            panel(S, E, g, p, g < 2)
        for g in range(4):
            for b in range(8):
                if g * 8 + b in (14, 15, 28, 29, 30, 31):
                    continue
                trail(S, E, g, p, b, g < 2)
    lane = lax.broadcasted_iota(jnp.int32, (K, K), 1)
    X = lambda i: get(E, i // 8, i % 8)
    U = lambda i: jnp.where(lax.broadcasted_iota(jnp.int32, (K, K), 0) <= lane, get(S, i // 8, i % 8), 0.0)
    scale = math.sqrt(256)
    for s in range(2):
        keep = jnp.where(lane < ranks[0], scale, 0.0)
        for l in range(2):
            x = X(s * 2 + l)
            for half in range(2):
                leaf_out[s, l, pl.ds(half * K, K), :] = (exact_nt(wide[s, l, half * K:half * K + K, :], x) * keep).astype(BF16)
        for j in range(5):
            keep = jnp.where(lane < ranks[j + 1], scale, 0.0)
            own = U(16 + s) if j == 0 else U(4 + s * 5 + j - 1)
            other = U(18 + s * 5 + j)
            x = X(4 + s * 5 + j)
            up = bits[j]
            tr_out[s, 0, j, pl.ds(pl.multiple_of(up * K, K), K), :] = (exact_nt(own, x) * keep).astype(BF16)
            tr_out[s, 0, j, pl.ds(pl.multiple_of((1 - up) * K, K), K), :] = (exact_nt(other, x) * keep).astype(BF16)

def finish(bits, ranks, wide, gram, chain, sib):
    vm = pl.BlockSpec(memory_space=pltpu.VMEM)
    sm = pl.BlockSpec(memory_space=pltpu.SMEM)
    return pl.pallas_call(
        kernel,
        out_shape=(jax.ShapeDtypeStruct((2, 2, 256, K), BF16), jax.ShapeDtypeStruct((2, 1, 5, 256, K), BF16)),
        in_specs=[sm, sm, vm, vm, vm, vm],
        out_specs=(vm, vm),
        scratch_shapes=[pltpu.VMEM((4 * 1024, K), F32), pltpu.VMEM((2 * 1024, K), F32)],
        compiler_params=pltpu.CompilerParams(vmem_limit_bytes=48 << 20),
    )(bits, ranks, wide, gram, chain, sib)


def dot(a, b):
    return jnp.dot(a, b, preferred_element_type=F32)


def dot_nt(a, b):
    return lax.dot_general(a, b, (((1,), (1,)), ((), ())), preferred_element_type=F32)


def halves(x):
    return [v.astype(BF16) for v in pieces(x)]


def remote(src, dst, send, recv, row, col):
    return pltpu.make_async_remote_copy(
        src_ref=src, dst_ref=dst, send_sem=send, recv_sem=recv,
        device_id=(row, col), device_id_type=pl.DeviceIdType.MESH,
    )


def sketch_kernel(
    lidx, blocks, samples, probes, compress,
    wide_out, gram_out, chain_out, sib_out,
    S, T1, T3, TO, TI, VP, RO, RI, WO, WI, CH, SB,
    own_sem, xs_send, xs_recv, zs_send, zs_recv, t_send, t_recv, r_send, r_recv, w_send, w_recv, b_send, b_recv,
):
    row, col = lax.axis_index("row"), lax.axis_index("col")
    rows, cols = lax.axis_size("row"), lax.axis_size("col")
    around = [(row + rows - 1) % rows, (row + 1) % rows]
    peer = [(col + s) % cols for s in range(4)]
    source = [(col + cols - s) % cols for s in range(4)]
    bit = lambda x, n: x // (1 << n) % 2
    flip = lambda x, n: x + (1 << n) * (1 - 2 * bit(x, n))
    mates = [(row, flip(col, 0)), (row, flip(col, 1))] + [(flip(row, n), col) for n in range(3)]

    barrier = pltpu.get_barrier_semaphore()
    greet = [(row, peer[s]) for s in (1, 2, 3)] + [(r, col) for r in around] + mates[3:]
    for device in greet:
        pl.semaphore_signal(barrier, inc=1, device_id=device, device_id_type=pl.DeviceIdType.MESH)
    pl.semaphore_wait(barrier, len(greet))

    part = lambda c: pl.ds(pl.multiple_of(64 * c, 64), 64)
    pair = lambda q: pl.ds(2 * q, 2)
    gather = {}
    for s in (2, 1, 3):
        gather[s] = remote(samples, S.at[pl.ds(8, 8), part(col)], xs_send.at[s], xs_recv.at[s], row, peer[s])
        gather[s].start()
    spread = {}
    for d in (0, 1):
        spread[d, 0] = remote(samples, S.at[pl.ds(16 - 16 * d, 8), part(col)], zs_send.at[d, 0], zs_recv.at[d, 0], around[d], col)
        spread[d, 0].start()
    own = pltpu.make_async_copy(samples, S.at[pl.ds(8, 8), part(col)], own_sem)
    own.start()

    ch, cm, cl = halves(compress[...])
    ct = jnp.concatenate(halves(compress[...].T), axis=1)
    left = []
    for i in range(8):
        p = probes[i]
        zt = dot_nt(ct, jnp.concatenate([p, p, p], axis=1))
        left.append(jnp.concatenate(halves(zt), axis=1))
    def term(i, k):
        b = blocks[i, k]
        return dot(left[i], jnp.concatenate([b, b, b], axis=0))
    for i in range(8):
        T1[i] = term(i, 1)
        T3[i] = term(i, 3)
    on = lambda i, k, j: jnp.where(lidx[i, k] == j, 1.0, 0.0).astype(F32)
    for j in range(8):
        up = term(j, 0)
        for i in range(j):
            up = up + on(i, 1, j) * T1[i]
        TO[0, j] = up
        down = term(j, 4)
        for i in range(j + 1, 8):
            down = down + on(i, 3, 16 + j) * T3[i]
        TO[1, j] = down
    order = (2, 1, 3, 0)
    terms = {}
    for s in order:
        for d in (0, 1):
            terms[d, s] = remote(TO.at[d, pair(peer[s])], TI.at[1 - d, pair(peer[s])], t_send.at[d, s], t_recv.at[1 - d, s], around[d], col)
            terms[d, s].start()
    for j in range(8):
        mid = term(j, 2)
        for i in range(j + 1, 8):
            mid = mid + on(i, 1, 8 + j) * T1[i]
        for i in range(j):
            mid = mid + on(i, 3, 8 + j) * T3[i]
        VP[j] = mid

    for s in (1, 3, 2):
        gather[s].wait_recv()
        for d in (0, 1):
            here = S.at[pl.ds(8, 8), part(source[s])]
            there = S.at[pl.ds(16 - 16 * d, 8), part(source[s])]
            spread[d, s] = remote(here, there, zs_send.at[d, s], zs_recv.at[d, s], around[d], col)
            spread[d, s].start()

    has = [jnp.where(row > 0, 1.0, 0.0).astype(F32), jnp.where(row < rows - 1, 1.0, 0.0).astype(F32)]
    reduce = {}
    for s in order:
        for d in (0, 1):
            remote(TO.at[d, pair(peer[s])], TI.at[d, pair(peer[s])], t_send.at[d, s], t_recv.at[d, s], around[d], col).wait_recv()
        total = VP[pair(peer[s])] + has[0] * TI[0, pair(peer[s])] + has[1] * TI[1, pair(peer[s])]
        RO[s] = total
        if s:
            reduce[s] = remote(RO.at[s], RI.at[s], r_send.at[s], r_recv.at[s], row, peer[s])
            reduce[s].start()

    own.wait()
    for s in (0, 1, 3, 2):
        for d in (0, 1):
            remote(samples, S.at[pl.ds(16 * d, 8), part(source[s])], zs_send.at[d, s], zs_recv.at[1 - d, s], around[d], col).wait_recv()
    cc = jnp.concatenate([ch, cm, cl, ch, cm, ch], axis=0)
    share = {}
    for s in order:
        acc = []
        for e in range(2):
            n = 2 * peer[s] + e
            total = dot(blocks[n, 2], S[8 + n])
            total = total + has[0] * dot(blocks[n, 0], S[n])
            total = total + has[1] * dot(blocks[n, 4], S[16 + n])
            for k, d in ((1, 0), (3, 1)):
                where = lidx[n, k]
                outside = jnp.where(where < 8, has[0], jnp.where(where >= 16, has[1], 1.0))
                total = total + outside * dot(blocks[n, k], S[where])
            acc.append(total)
        h, m, l = halves(jnp.concatenate(acc, axis=0))
        w = dot(jnp.concatenate([h, h, h, m, m, l], axis=1), cc)
        WO[s] = w.reshape(2, 64, K)
        if s:
            share[s] = remote(WO.at[s], WI.at[:, part(col)], w_send.at[s], w_recv.at[s], row, peer[s])
            share[s].start()
        else:
            WI[:, part(col)] = w.reshape(2, 64, K)

    for s in (1, 3, 2):
        reduce[s].wait_recv()
    for l in range(2):
        vt = RO[0, l] + RI[1, l] + RI[3, l] + RI[2, l]
        wide_out[1, l] = vt.T
        gram_out[1, l] = exact_nt(vt, vt)
    for s in (1, 3, 2):
        share[s].wait_recv()
    for l in range(2):
        wt = WI[l].T
        wide_out[0, l] = WI[l]
        gram_out[0, l] = exact_nt(wt, wt)
    for side in range(2):
        CH[0, side] = gram_out[side, 0] + gram_out[side, 1]
    swaps = []
    for j in range(5):
        swaps.append(remote(CH.at[j], SB.at[j], b_send.at[j], b_recv.at[j], *mates[j]))
        swaps[j].start()
        swaps[j].wait_recv()
        CH[j + 1] = CH[j] + SB[j]
    for j in range(6):
        chain_out[j] = CH[j]
    for j in range(5):
        sib_out[j] = SB[j]
    for copies in (gather, spread, terms, reduce, share):
        for c in copies.values():
            c.wait_send()
    for c in swaps:
        c.wait_send()


def sketch(lidx, blocks, samples, probes, compress):
    vm = pl.BlockSpec(memory_space=pltpu.VMEM)
    sm = pl.BlockSpec(memory_space=pltpu.SMEM)
    dma = pltpu.SemaphoreType.DMA
    shape = jax.ShapeDtypeStruct
    return pl.pallas_call(
        sketch_kernel,
        out_shape=(
            shape((2, 2, 256, K), F32), shape((2, 2, K, K), F32),
            shape((6, 2, K, K), F32), shape((5, 2, K, K), F32),
        ),
        in_specs=[sm, vm, vm, vm, vm],
        out_specs=(vm, vm, vm, vm),
        scratch_shapes=[
            pltpu.VMEM((24, 256, 256), BF16),
            pltpu.VMEM((8, K, 256), F32), pltpu.VMEM((8, K, 256), F32),
            pltpu.VMEM((2, 8, K, 256), F32), pltpu.VMEM((2, 8, K, 256), F32),
            pltpu.VMEM((8, K, 256), F32),
            pltpu.VMEM((4, 2, K, 256), F32), pltpu.VMEM((4, 2, K, 256), F32),
            pltpu.VMEM((4, 2, 64, K), F32), pltpu.VMEM((2, 256, K), F32),
            pltpu.VMEM((6, 2, K, K), F32), pltpu.VMEM((5, 2, K, K), F32),
            dma, dma((4,)), dma((4,)), dma((2, 4)), dma((2, 4)), dma((2, 4)), dma((2, 4)),
            dma((4,)), dma((4,)), dma((4,)), dma((4,)), dma((5,)), dma((5,)),
        ],
        compiler_params=pltpu.CompilerParams(
            collective_id=0, has_side_effects=True, vmem_limit_bytes=48 << 20
        ),
    )(lidx, blocks, samples, probes, compress)


def body(blocks, samples, probes, compress, pattern, ranks):
    row_index = lax.axis_index("row")
    col_index = lax.axis_index("col")
    n_blocks = blocks.shape[0]
    local_index = pattern - row_index * n_blocks + n_blocks
    wide, gram, chain, sib = sketch(local_index, blocks, samples, probes, compress)
    bits = jnp.stack([i >> n & 1 for i, n in ((col_index, 0), (col_index, 1), (row_index, 0), (row_index, 1), (row_index, 2))])
    return finish(bits, ranks, wide, gram, chain, sib)


def solution(mesh):
    return jax.shard_map(
        body,
        mesh=mesh,
        in_specs=(
            P("row", None, "col", None),
            P("row", "col", None),
            P("row", "col", None),
            P(),
            P("row", None),
            P(),
        ),
        out_specs=(P(None, ("row", "col"), None, None), P(None, ("row", "col"), None, None, None)),
        check_vma=False,
    )
```

```python
import math

import jax
import jax.numpy as jnp
from jax import lax
from jax.experimental import pallas as pl
from jax.experimental.pallas import tpu as pltpu
from jax.sharding import PartitionSpec as P

K = 128
F32 = jnp.float32
BF16 = jnp.bfloat16

def pieces(x):
    h = x.astype(BF16).astype(F32)
    r = x - h
    m = r.astype(BF16).astype(F32)
    return h, m, r - m

def panel(S, E, g, p, with_e):
    base = (g * 16 + p) * 64
    rows = [S[pl.ds(base + r, 8, stride=8), :] for r in range(8)]
    erows = [E[pl.ds(base + r, 8, stride=8), :] for r in range(8)] if with_e else None
    a = {}
    for r in range(8):
        for k in range(r, 8):
            c = 8 * p + k
            a[r, k] = jnp.broadcast_to(rows[r][:, c:c + 1], (8, K))
    for r in range(8):
        inv = lax.rsqrt(a[r, r])
        u = {k: a[r, k] * inv for k in range(r + 1, 8)}
        rows[r] = rows[r] * inv
        if with_e:
            erows[r] = erows[r] * inv
        for i in range(r + 1, 8):
            for k in range(i, 8):
                a[i, k] = a[i, k] - u[i] * u[k]
            rows[i] = rows[i] - u[i] * rows[r]
            if with_e:
                erows[i] = erows[i] - u[i] * erows[r]
    for r in range(8):
        S[pl.ds(base + r, 8, stride=8), :] = rows[r]
        if with_e:
            E[pl.ds(base + r, 8, stride=8), :] = erows[r]

def trail(S, E, g, p, b, with_e):
    if p == 15:
        return
    at = lambda q: pl.ds(((g * 16 + q) * 8 + b) * 8, 8)
    h, m, l = pieces(S[at(p), :])
    first = (8 * (p + 1)) // 16 * 16
    left = jnp.concatenate([h, h, h, m, m, l], axis=0).T[first:].astype(BF16)
    right = jnp.concatenate([h, m, l, h, m, h], axis=0)
    if with_e:
        h, m, l = pieces(E[at(p), :])
        right = jnp.concatenate([right, jnp.concatenate([h, m, l, h, m, h], axis=0)], axis=1)
    t = jnp.dot(left, right.astype(BF16), preferred_element_type=F32)
    for q in range(p + 1, 16):
        o = 8 * q - first
        S[at(q), :] = S[at(q), :] - t[o:o + 8, :K]
        if with_e:
            E[at(q), :] = E[at(q), :] - t[o:o + 8, K:]

def get(ref, g, b):
    return jnp.concatenate([ref[pl.ds(((g * 16 + q) * 8 + b) * 8, 8), :] for q in range(16)], axis=0)

def put(ref, g, b, x):
    for q in range(16):
        ref[pl.ds(((g * 16 + q) * 8 + b) * 8, 8), :] = x[8 * q:8 * q + 8]

def cat(x, order):
    h, m, l = x
    d = {"h": h, "m": m, "l": l}
    return jnp.concatenate([d[c] for c in order], axis=1)

def exact_nt(x, y):
    a = cat([v.astype(BF16) for v in pieces(x)], "hhmhml")
    b = cat([v.astype(BF16) for v in pieces(y)], "hmhlmh")
    return lax.dot_general(a, b, (((1,), (1,)), ((), ())), preferred_element_type=F32)


def dot(a, b):
    return jnp.dot(a, b, preferred_element_type=F32)


def dot_nt(a, b):
    return lax.dot_general(a, b, (((1,), (1,)), ((), ())), preferred_element_type=F32)


def halves(x):
    return [v.astype(BF16) for v in pieces(x)]


def remote(src, dst, send, recv, row, col):
    return pltpu.make_async_remote_copy(
        src_ref=src, dst_ref=dst, send_sem=send, recv_sem=recv,
        device_id=(row, col), device_id_type=pl.DeviceIdType.MESH,
    )


def sketch_kernel(
    lidx, ranks, lpad, blocks, samples, probes, compress,
    leaf_out, tr_out,
    S, BL, PR, CM, NB, NP, NL, NS, T1, T3, RO, RI, WS, PO, PI, WO, WI, CH, XG, CG, ZG, FO, FI, WD, GR, CS, CE,
    l_sem, n_sem, xs_send, xs_recv, z_send, z_recv, p_send, p_recv, r_send, r_recv, w_send, w_recv, b_send, b_recv,
):
    row, col = lax.axis_index("row"), lax.axis_index("col")
    rows, cols = lax.axis_size("row"), lax.axis_size("col")
    around = [(row + rows - 1) % rows, (row + 1) % rows]
    peer = [(col + s) % cols for s in range(4)]
    flip = lambda x, n: x + (1 << n) * (1 - 2 * (x // (1 << n) % 2))
    x_mates = [None, flip(col, 0), flip(col, 1), flip(flip(col, 0), 1)]
    z_mates = [None, flip(row, 1), flip(row, 2), flip(flip(row, 1), 2)]
    core_mate = flip(row, 0)

    barrier = pltpu.get_barrier_semaphore()
    greet = [(row, peer[s]) for s in (1, 2, 3)] + [(r, col) for r in around] + [(r, col) for r in z_mates[1:]]
    for device in greet:
        pl.semaphore_signal(barrier, inc=1, device_id=device, device_id_type=pl.DeviceIdType.MESH)
    local = [
        pltpu.make_async_copy(blocks, BL, l_sem.at[0]),
        pltpu.make_async_copy(probes, PR, l_sem.at[1]),
        pltpu.make_async_copy(samples, S.at[:, pl.ds(pl.multiple_of(64 * col, 64), 64)], l_sem.at[2]),
        pltpu.make_async_copy(compress, CM, l_sem.at[3]),
    ]
    for c in local:
        c.start()
    pl.semaphore_wait(barrier, len(greet))

    part = lambda c: pl.ds(pl.multiple_of(64 * c, 64), 64)
    pair = lambda q: pl.ds(2 * q, 2)
    sent = []
    def send(*args):
        c = remote(*args)
        c.start()
        sent.append(c)
        return c
    gather = {s: send(samples, S.at[:, part(col)], xs_send.at[s], xs_recv.at[s], row, peer[s]) for s in (2, 1, 3)}
    near = []
    for n in range(4):
        for d in (0, 1):
            full, crossing = ((0, 1), (4, 3))[d]
            source, target = (
                (lpad, NL.at[1 - d]),
                (blocks.at[:, full], NB.at[1 - d, 0]),
                (blocks.at[:, crossing], NB.at[1 - d, 1]),
                (probes, NP.at[1 - d]),
            )[n]
            near.append(send(source, target, z_send.at[d, n], z_recv.at[1 - d, n], around[d], col))

    def flat(p):
        zt = dot_nt(ct, jnp.concatenate([p, p, p], axis=1))
        return jnp.concatenate(halves(zt), axis=1)
    def term(a, b):
        return dot(a, jnp.concatenate([b, b, b], axis=0))
    one = lambda c: jnp.where(c, 1.0, 0.0).astype(F32)
    for c in local:
        c.wait()
    ch, cm, cl = halves(CM[...])
    ct = jnp.concatenate(halves(CM[...].T), axis=1)
    left = [flat(PR[i]) for i in range(8)]
    for i in range(8):
        T1[i] = term(left[i], BL[i, 1])
        T3[i] = term(left[i], BL[i, 3])
    for j in range(8):
        mid = term(left[j], BL[j, 2])
        for i in range(j + 1, 8):
            mid = mid + one(lidx[i, 1] == 8 + j) * T1[i]
        for i in range(j):
            mid = mid + one(lidx[i, 3] == 8 + j) * T3[i]
        RO[j] = mid

    has = [one(row > 0), one(row < rows - 1)]
    def behind_of(d):
        return (row + rows + 2 * d - 1) % rows
    def arrived(n, d):
        source, target = (
            (lpad, NL.at[d]),
            (blocks.at[:, 0], NB.at[d, 0]),
            (blocks.at[:, 0], NB.at[d, 1]),
            (probes, NP.at[d]),
        )[n]
        remote(source, target, z_send.at[d, n], z_recv.at[d, n], behind_of(d), col).wait_recv()
    def column_of(d, n):
        return NS[d, n, 3 - 2 * d] - 16 * (1 - d)
    def indices(d):
        arrived(0, d)
        copy = pltpu.make_async_copy(NL.at[d], NS.at[d], n_sem.at[d])
        copy.start()
        copy.wait()
    def terms(d):
        exists = jnp.where(d == 0, has[0], has[1])
        left = [flat(NP[d, i]) for i in range(8)]
        for i in range(8):
            T1[i] = exists * term(left[i], NB[d, 1, i])
        for j in range(8):
            total = RO[j] + exists * term(left[j], NB[d, 0, j])
            for i in range(8):
                if i != j:
                    total = total + one(column_of(d, i) == j) * T1[i]
            RO[j] = total
    def products(d):
        for q in range(4):
            acc = []
            for n in (2 * q, 2 * q + 1):
                where = column_of(d, n)
                index = jnp.clip(where, 0, 7)
                acc.append(dot(NB[d, 0, n], S[n]) + one(where == index) * dot(NB[d, 1, n], S[index]))
            PO[d, 2 * q:2 * q + 2] = squeeze(acc)
        send(PO.at[d], PI.at[1 - d], p_send.at[d], p_recv.at[1 - d], behind_of(d), col)
    core = row % 2
    beside, away = 1 - core, core
    for n in (1, 2, 3):
        arrived(n, beside)
    indices(beside)
    terms(beside)
    cc = jnp.concatenate([ch, cm, cl, ch, cm, ch], axis=0)
    def squeeze(acc):
        h, m, l = halves(jnp.concatenate(acc, axis=0))
        return dot(jnp.concatenate([h, h, h, m, m, l], axis=1), cc).reshape(len(acc), 64, K)
    for s in (1, 3, 2):
        gather[s].wait_recv()
    for q in range(4):
        acc = []
        for n in (2 * q, 2 * q + 1):
            behind, ahead = lidx[n, 1], lidx[n, 3]
            total = dot(BL[n, 2], S[n])
            total = total + one(behind >= 8) * dot(BL[n, 1], S[jnp.clip(behind - 8, 0, 7)])
            total = total + one(ahead < 16) * dot(BL[n, 3], S[jnp.clip(ahead - 8, 0, 7)])
            acc.append(total)
        WS[2 * q:2 * q + 2] = squeeze(acc)

    products(beside)
    indices(away)
    for n in (1, 2):
        arrived(n, away)
    products(away)
    arrived(3, away)
    terms(away)
    order = (2, 1, 3)
    reduce = {s: send(RO.at[pair(peer[s])], RI.at[s], r_send.at[s], r_recv.at[s], row, peer[s]) for s in order}

    for d in (0, 1):
        remote(PO.at[d], PI.at[d], p_send.at[d], p_recv.at[d], around[d], col).wait_recv()
    share = {}
    for s in (2, 1, 3, 0):
        q = pair(peer[s])
        w = WS[q] + has[0] * PI[0, q] + has[1] * PI[1, q]
        if s:
            WO[s] = w
            share[s] = send(WO.at[s], WI.at[:, part(col)], w_send.at[s], w_recv.at[s], row, peer[s])
        else:
            WI[:, part(col)] = w

    for s in (1, 3, 2):
        reduce[s].wait_recv()
    for l in range(2):
        vt = RO[2 * col + l] + RI[1, l] + RI[3, l] + RI[2, l]
        WD[1, l] = vt.T
        GR[1, l] = exact_nt(vt, vt)
    for s in (1, 3, 2):
        share[s].wait_recv()
    for l in range(2):
        wt = WI[l].T
        WD[0, l] = WI[l]
        GR[0, l] = exact_nt(wt, wt)

    square = (K, K)
    lane = lax.broadcasted_iota(jnp.int32, square, 1)
    below = lax.broadcasted_iota(jnp.int32, square, 0)
    eye = one(below == lane)
    def factor(groups):
        for g, members in groups:
            for b in range(8):
                put(CS, g, b, members[b][0] if b < len(members) else eye)
                put(CE, g, b, eye)
        for p in range(16):
            for g, members in groups:
                panel(CS, CE, g, p, True)
            for g, members in groups:
                for b, (unused, inverse) in enumerate(members):
                    trail(CS, CE, g, p, b, inverse)
    upper = lambda g, b: jnp.where(below <= lane, get(CS, g, b), 0.0)
    keep = lambda n: jnp.where(lane < ranks[n], math.sqrt(256), 0.0)
    bits = [col % 2, col // 2 % 2, row % 2, row // 2 % 2, row // 4 % 2]
    def merge(j, own, sibling, parent):
        for s in range(2):
            x = get(CE, *parent[s])
            for where, slot in ((bits[j], own[s]), (1 - bits[j], sibling[s])):
                rows_at = pl.ds(pl.multiple_of(where * K, K), K)
                tr_out[s, 0, j, rows_at, :] = (exact_nt(upper(*slot), x) * keep(j + 1)).astype(BF16)

    for side in range(2):
        CH[0, side] = GR[side, 0] + GR[side, 1]
    step = {x: send(CH.at[0], XG.at[x], b_send.at[x], b_recv.at[x], row, x_mates[x]) for x in (2, 3, 1)}
    factor([(0, [(GR[s, l], True) for s in range(2) for l in range(2)] + [(CH[0, s], False) for s in range(2)])])
    for s in range(2):
        for l in range(2):
            x = get(CE, 0, 2 * s + l)
            for half in range(2):
                at = slice(half * K, half * K + K)
                leaf_out[s, l, at, :] = (exact_nt(WD[s, l, at, :], x) * keep(0)).astype(BF16)
    for x in (1, 2, 3):
        step[x].wait_recv()
    first = CH[0] + XG[1]
    second = XG[2] + XG[3]
    CH[1] = first + second
    joined = send(CH.at[1], CG, b_send.at[4], b_recv.at[4], core_mate, col)
    joined.wait_recv()
    third = CG[...]
    CH[2] = CH[1] + third
    mine, other = row % 2, 1 - row % 2
    step = {x: send(CH.at[2, mine], ZG.at[x], b_send.at[4 + x], b_recv.at[4 + x], z_mates[x], col) for x in (3, 2, 1)}
    factor([
        (1, [(XG[1, s], False) for s in range(2)] + [(second[s], False) for s in range(2)]
            + [(first[s], True) for s in range(2)] + [(CH[1, s], True) for s in range(2)]),
        (2, [(third[s], False) for s in range(2)] + [(CH[2, s], True) for s in range(2)]),
    ])
    for x in (1, 2, 3):
        step[x].wait_recv()
    FO[0] = ZG[1]
    FO[1] = ZG[2] + ZG[3]
    last = send(FO, FI, b_send.at[0], b_recv.at[0], core_mate, col)
    merge(0, [(0, 4), (0, 5)], [(1, 0), (1, 1)], [(1, 4), (1, 5)])
    merge(1, [(1, 4), (1, 5)], [(1, 2), (1, 3)], [(1, 6), (1, 7)])
    merge(2, [(1, 6), (1, 7)], [(2, 0), (2, 1)], [(2, 2), (2, 3)])
    last.wait_recv()
    swap = row % 2 == 1
    fourth = [jnp.where(swap, FI[0], FO[0]), jnp.where(swap, FO[0], FI[0])]
    fifth = [jnp.where(swap, FI[1], FO[1]), jnp.where(swap, FO[1], FI[1])]
    level = [CH[2, s] + fourth[s] for s in range(2)]
    factor([(3, [(v, False) for v in fourth + fifth] + [(v, True) for v in level] + [(level[s] + fifth[s], True) for s in range(2)])])
    merge(3, [(2, 2), (2, 3)], [(3, 0), (3, 1)], [(3, 4), (3, 5)])
    merge(4, [(3, 4), (3, 5)], [(3, 2), (3, 3)], [(3, 6), (3, 7)])
    for c in sent:
        c.wait_send()


def sketch(lidx, ranks, lpad, blocks, samples, probes, compress):
    vm = pl.BlockSpec(memory_space=pltpu.VMEM)
    sm = pl.BlockSpec(memory_space=pltpu.SMEM)
    hbm = pl.BlockSpec(memory_space=pltpu.HBM)
    dma = pltpu.SemaphoreType.DMA
    shape = jax.ShapeDtypeStruct
    return pl.pallas_call(
        sketch_kernel,
        out_shape=(
            shape((2, 2, 256, K), BF16), shape((2, 1, 5, 256, K), BF16),
        ),
        in_specs=[sm, sm, vm, hbm, hbm, hbm, hbm],
        out_specs=(vm, vm),
        scratch_shapes=[
            pltpu.VMEM((8, 256, 256), BF16),
            pltpu.VMEM((8, 5, 64, 256), BF16), pltpu.VMEM((8, 64, 256), BF16), pltpu.VMEM((256, K), F32),
            pltpu.VMEM((2, 2, 8, 64, 256), BF16), pltpu.VMEM((2, 8, 64, 256), BF16),
            pltpu.VMEM((2, 8, K), jnp.int32), pltpu.SMEM((2, 8, K), jnp.int32),
            pltpu.VMEM((8, K, 256), F32), pltpu.VMEM((8, K, 256), F32),
            pltpu.VMEM((8, K, 256), F32), pltpu.VMEM((4, 2, K, 256), F32),
            pltpu.VMEM((8, 64, K), F32), pltpu.VMEM((2, 8, 64, K), F32), pltpu.VMEM((2, 8, 64, K), F32),
            pltpu.VMEM((4, 2, 64, K), F32), pltpu.VMEM((2, 256, K), F32),
            pltpu.VMEM((3, 2, K, K), F32), pltpu.VMEM((4, 2, K, K), F32), pltpu.VMEM((2, K, K), F32),
            pltpu.VMEM((4, K, K), F32), pltpu.VMEM((2, K, K), F32), pltpu.VMEM((2, K, K), F32),
            pltpu.VMEM((2, 2, 256, K), F32), pltpu.VMEM((2, 2, K, K), F32),
            pltpu.VMEM((4096, K), F32), pltpu.VMEM((4096, K), F32),
            dma((4,)), dma((2,)), dma((4,)), dma((4,)), dma((2, 4)), dma((2, 4)), dma((2,)), dma((2,)),
            dma((4,)), dma((4,)), dma((4,)), dma((4,)), dma((8,)), dma((8,)),
        ],
        compiler_params=pltpu.CompilerParams(
            collective_id=0, has_side_effects=True, vmem_limit_bytes=60 << 20
        ),
    )(lidx, ranks, lpad, blocks, samples, probes, compress)


def body(blocks, samples, probes, compress, pattern, ranks):
    n_blocks = blocks.shape[0]
    local_index = pattern - lax.axis_index("row") * n_blocks + n_blocks
    padded_index = jnp.pad(local_index, ((0, 0), (0, compress.shape[1] - local_index.shape[1])))
    return sketch(local_index, ranks, padded_index, blocks, samples, probes, compress)


def solution(mesh):
    return jax.shard_map(
        body,
        mesh=mesh,
        in_specs=(
            P("row", None, "col", None),
            P("row", "col", None),
            P("row", "col", None),
            P(),
            P("row", None),
            P(),
        ),
        out_specs=(P(None, ("row", "col"), None, None), P(None, ("row", "col"), None, None, None)),
        check_vma=False,
    )
```

```python
import math

import jax
import jax.numpy as jnp
from jax import lax
from jax.experimental import pallas as pl
from jax.experimental.pallas import tpu as pltpu
from jax.sharding import PartitionSpec as P

K = 128
F32 = jnp.float32
BF16 = jnp.bfloat16

def pieces(x):
    h = x.astype(BF16).astype(F32)
    r = x - h
    m = r.astype(BF16).astype(F32)
    return h, m, r - m

def panel(S, E, g, p, with_e):
    base = (g * 16 + p) * 64
    rows = [S[pl.ds(base + r, 8, stride=8), :] for r in range(8)]
    erows = [E[pl.ds(base + r, 8, stride=8), :] for r in range(8)] if with_e else None
    a = {}
    for r in range(8):
        for k in range(r, 8):
            c = 8 * p + k
            a[r, k] = jnp.broadcast_to(rows[r][:, c:c + 1], (8, K))
    for r in range(8):
        inv = lax.rsqrt(a[r, r])
        u = {k: a[r, k] * inv for k in range(r + 1, 8)}
        rows[r] = rows[r] * inv
        if with_e:
            erows[r] = erows[r] * inv
        for i in range(r + 1, 8):
            for k in range(i, 8):
                a[i, k] = a[i, k] - u[i] * u[k]
            rows[i] = rows[i] - u[i] * rows[r]
            if with_e:
                erows[i] = erows[i] - u[i] * erows[r]
    for r in range(8):
        S[pl.ds(base + r, 8, stride=8), :] = rows[r]
        if with_e:
            E[pl.ds(base + r, 8, stride=8), :] = erows[r]

def trail(S, E, g, p, b, with_e):
    if p == 15:
        return
    at = lambda q: pl.ds(((g * 16 + q) * 8 + b) * 8, 8)
    h, m, l = pieces(S[at(p), :])
    first = (8 * (p + 1)) // 16 * 16
    left = jnp.concatenate([h, h, h, m, m, l], axis=0).T[first:].astype(BF16)
    right = jnp.concatenate([h, m, l, h, m, h], axis=0)
    if with_e:
        h, m, l = pieces(E[at(p), :])
        right = jnp.concatenate([right, jnp.concatenate([h, m, l, h, m, h], axis=0)], axis=1)
    t = jnp.dot(left, right.astype(BF16), preferred_element_type=F32)
    for q in range(p + 1, 16):
        o = 8 * q - first
        S[at(q), :] = S[at(q), :] - t[o:o + 8, :K]
        if with_e:
            E[at(q), :] = E[at(q), :] - t[o:o + 8, K:]

def get(ref, g, b):
    return jnp.concatenate([ref[pl.ds(((g * 16 + q) * 8 + b) * 8, 8), :] for q in range(16)], axis=0)

def put(ref, g, b, x):
    for q in range(16):
        ref[pl.ds(((g * 16 + q) * 8 + b) * 8, 8), :] = x[8 * q:8 * q + 8]

def cat(x, order):
    h, m, l = x
    d = {"h": h, "m": m, "l": l}
    return jnp.concatenate([d[c] for c in order], axis=1)

def exact_nt(x, y):
    a = cat([v.astype(BF16) for v in pieces(x)], "hhmhml")
    b = cat([v.astype(BF16) for v in pieces(y)], "hmhlmh")
    return lax.dot_general(a, b, (((1,), (1,)), ((), ())), preferred_element_type=F32)


def dot(a, b):
    return jnp.dot(a, b, preferred_element_type=F32)


def dot_nt(a, b):
    return lax.dot_general(a, b, (((1,), (1,)), ((), ())), preferred_element_type=F32)


def halves(x):
    return [v.astype(BF16) for v in pieces(x)]


def remote(src, dst, send, recv, row, col):
    return pltpu.make_async_remote_copy(
        src_ref=src, dst_ref=dst, send_sem=send, recv_sem=recv,
        device_id=(row, col), device_id_type=pl.DeviceIdType.MESH,
    )


def sketch_kernel(
    pattern, ranks, names, blocks, samples, probes, compress,
    leaf_out, tr_out,
    S, BL, PR, CM, LP, NB, NP, NL, NS, T1, T3, RO, RI, WS, PO, PI, WO, WI, CH, XG, CG, ZG, FO, FI, WD, GR, CS, CE,
    l_sem, n_sem, xs_send, xs_recv, z_send, z_recv, p_send, p_recv, r_send, r_recv, w_send, w_recv, b_send, b_recv,
):
    row, col = lax.axis_index("row"), lax.axis_index("col")
    rows, cols = lax.axis_size("row"), lax.axis_size("col")
    around = [(row + rows - 1) % rows, (row + 1) % rows]
    peer = [(col + s) % cols for s in range(4)]
    flip = lambda x, n: x + (1 << n) * (1 - 2 * (x // (1 << n) % 2))
    x_mates = [None, flip(col, 0), flip(col, 1), flip(flip(col, 0), 1)]
    z_mates = [None, flip(row, 1), flip(row, 2), flip(flip(row, 1), 2)]
    core_mate = flip(row, 0)

    base = 8 * row

    barrier = pltpu.get_barrier_semaphore()
    greet = [(row, peer[s]) for s in (1, 2, 3)] + [(r, col) for r in around] + [(r, col) for r in z_mates[1:]]
    for device in greet:
        pl.semaphore_signal(barrier, inc=1, device_id=device, device_id_type=pl.DeviceIdType.MESH)
    local = [
        pltpu.make_async_copy(blocks, BL, l_sem.at[0]),
        pltpu.make_async_copy(probes, PR, l_sem.at[1]),
        pltpu.make_async_copy(samples, S.at[:, pl.ds(pl.multiple_of(64 * col, 64), 64)], l_sem.at[2]),
        pltpu.make_async_copy(compress, CM, l_sem.at[3]),
    ]
    for c in local:
        c.start()
    LP[...] = jnp.zeros_like(LP)
    LP[:, :5] = names[...]
    pl.semaphore_wait(barrier, len(greet))

    part = lambda c: pl.ds(pl.multiple_of(64 * c, 64), 64)
    pair = lambda q: pl.ds(2 * q, 2)
    sent = []
    def send(*args):
        c = remote(*args)
        c.start()
        sent.append(c)
        return c
    gather = {s: send(samples, S.at[:, part(col)], xs_send.at[s], xs_recv.at[s], row, peer[s]) for s in (2, 1, 3)}
    def to_neighbours(n):
        for d in (0, 1):
            full, crossing = ((0, 1), (4, 3))[d]
            source, target = (
                (LP, NL.at[1 - d]),
                (blocks.at[:, full], NB.at[1 - d, 0]),
                (blocks.at[:, crossing], NB.at[1 - d, 1]),
                (probes, NP.at[1 - d]),
            )[n]
            send(source, target, z_send.at[d, n], z_recv.at[1 - d, n], around[d], col)
    for n in range(3):
        to_neighbours(n)

    def flat(p):
        zt = dot_nt(ct, jnp.concatenate([p, p, p], axis=1))
        return jnp.concatenate(halves(zt), axis=1)
    def term(a, b):
        return dot(a, jnp.concatenate([b, b, b], axis=0))
    one = lambda c: jnp.where(c, 1.0, 0.0).astype(F32)
    for c in local:
        c.wait()
    ch, cm, cl = halves(CM[...])
    ct = jnp.concatenate(halves(CM[...].T), axis=1)
    left = [flat(PR[i]) for i in range(8)]
    for i in range(8):
        T1[i] = term(left[i], BL[i, 1])
        T3[i] = term(left[i], BL[i, 3])
    for j in range(8):
        mid = term(left[j], BL[j, 2])
        for i in range(j + 1, 8):
            mid = mid + one(pattern[i, 1] - base == j) * T1[i]
        for i in range(j):
            mid = mid + one(pattern[i, 3] - base == j) * T3[i]
        RO[j] = mid
        if j == 0:
            to_neighbours(3)

    has = [one(row > 0), one(row < rows - 1)]
    def behind_of(d):
        return (row + rows + 2 * d - 1) % rows
    def arrived(n, d):
        source, target = (
            (LP, NL.at[d]),
            (blocks.at[:, 0], NB.at[d, 0]),
            (blocks.at[:, 0], NB.at[d, 1]),
            (probes, NP.at[d]),
        )[n]
        remote(source, target, z_send.at[d, n], z_recv.at[d, n], behind_of(d), col).wait_recv()
    def column_of(d, n):
        return NS[d, n, 3 - 2 * d] - base
    def indices(d):
        arrived(0, d)
        copy = pltpu.make_async_copy(NL.at[d], NS.at[d], n_sem.at[d])
        copy.start()
        copy.wait()
    def terms(d):
        exists = jnp.where(d == 0, has[0], has[1])
        left = [flat(NP[d, i]) for i in range(8)]
        for i in range(8):
            T1[i] = exists * term(left[i], NB[d, 1, i])
        for j in range(8):
            total = RO[j] + exists * term(left[j], NB[d, 0, j])
            for i in range(8):
                if i != j:
                    total = total + one(column_of(d, i) == j) * T1[i]
            RO[j] = total
    def products(d):
        for q in range(4):
            acc = []
            for n in (2 * q, 2 * q + 1):
                where = column_of(d, n)
                index = jnp.clip(where, 0, 7)
                acc.append(dot(NB[d, 0, n], S[n]) + one(where == index) * dot(NB[d, 1, n], S[index]))
            PO[d, 2 * q:2 * q + 2] = squeeze(acc)
            send(PO.at[d, pair(q)], PI.at[1 - d, pair(q)], p_send.at[d, q], p_recv.at[1 - d, q], behind_of(d), col)
    core = row % 2
    beside, away = 1 - core, core
    for n in (1, 2, 3):
        arrived(n, beside)
    indices(beside)
    terms(beside)
    cc = jnp.concatenate([ch, cm, cl, ch, cm, ch], axis=0)
    def squeeze(acc):
        h, m, l = halves(jnp.concatenate(acc, axis=0))
        return dot(jnp.concatenate([h, h, h, m, m, l], axis=1), cc).reshape(len(acc), 64, K)
    for s in (1, 3, 2):
        gather[s].wait_recv()
    for q in range(4):
        acc = []
        for n in (2 * q, 2 * q + 1):
            total = dot(BL[n, 2], S[n])
            for k in (1, 3):
                where = pattern[n, k] - base
                index = jnp.clip(where, 0, 7)
                total = total + one(where == index) * dot(BL[n, k], S[index])
            acc.append(total)
        WS[2 * q:2 * q + 2] = squeeze(acc)

    products(beside)
    indices(away)
    for n in (1, 2):
        arrived(n, away)
    products(away)
    arrived(3, away)
    terms(away)
    order = (2, 1, 3)
    reduce = {s: send(RO.at[pair(peer[s])], RI.at[s], r_send.at[s], r_recv.at[s], row, peer[s]) for s in order}

    share = {}
    for s in (2, 1, 3, 0):
        q = pair(peer[s])
        for d in (0, 1):
            remote(PO.at[d, q], PI.at[d, q], p_send.at[d, peer[s]], p_recv.at[d, peer[s]], around[d], col).wait_recv()
        w = WS[q] + has[0] * PI[0, q] + has[1] * PI[1, q]
        if s:
            WO[s] = w
            share[s] = send(WO.at[s], WI.at[:, part(col)], w_send.at[s], w_recv.at[s], row, peer[s])
        else:
            WI[:, part(col)] = w

    for s in (1, 3, 2):
        reduce[s].wait_recv()
    for l in range(2):
        vt = RO[2 * col + l] + RI[1, l] + RI[3, l] + RI[2, l]
        WD[1, l] = vt.T
        GR[1, l] = exact_nt(vt, vt)
    for s in (1, 3, 2):
        share[s].wait_recv()
    for l in range(2):
        wt = WI[l].T
        WD[0, l] = WI[l]
        GR[0, l] = exact_nt(wt, wt)

    square = (K, K)
    lane = lax.broadcasted_iota(jnp.int32, square, 1)
    below = lax.broadcasted_iota(jnp.int32, square, 0)
    eye = one(below == lane)
    def factor(groups):
        for g, members in groups:
            for b in range(8):
                put(CS, g, b, members[b][0] if b < len(members) else eye)
                put(CE, g, b, eye)
        for p in range(16):
            for g, members in groups:
                panel(CS, CE, g, p, True)
            for g, members in groups:
                for b, (unused, inverse) in enumerate(members):
                    trail(CS, CE, g, p, b, inverse)
    upper = lambda g, b: jnp.where(below <= lane, get(CS, g, b), 0.0)
    keep = lambda n: jnp.where(lane < ranks[n], math.sqrt(256), 0.0)
    bits = [col % 2, col // 2 % 2, row % 2, row // 2 % 2, row // 4 % 2]
    def merge(j, own, sibling, parent):
        for s in range(2):
            x = get(CE, *parent[s])
            for where, slot in ((bits[j], own[s]), (1 - bits[j], sibling[s])):
                rows_at = pl.ds(pl.multiple_of(where * K, K), K)
                tr_out[s, 0, j, rows_at, :] = (exact_nt(upper(*slot), x) * keep(j + 1)).astype(BF16)

    for side in range(2):
        CH[0, side] = GR[side, 0] + GR[side, 1]
    step = {x: send(CH.at[0], XG.at[x], b_send.at[x], b_recv.at[x], row, x_mates[x]) for x in (2, 3, 1)}
    factor([(0, [(GR[s, l], True) for s in range(2) for l in range(2)] + [(CH[0, s], False) for s in range(2)])])
    for x in (1, 2, 3):
        step[x].wait_recv()
    first = CH[0] + XG[1]
    second = XG[2] + XG[3]
    CH[1] = first + second
    joined = send(CH.at[1], CG, b_send.at[4], b_recv.at[4], core_mate, col)
    for s in range(2):
        for l in range(2):
            x = get(CE, 0, 2 * s + l)
            for half in range(2):
                at = slice(half * K, half * K + K)
                leaf_out[s, l, at, :] = (exact_nt(WD[s, l, at, :], x) * keep(0)).astype(BF16)
    joined.wait_recv()
    third = CG[...]
    CH[2] = CH[1] + third
    mine, other = row % 2, 1 - row % 2
    step = {x: send(CH.at[2, mine], ZG.at[x], b_send.at[4 + x], b_recv.at[4 + x], z_mates[x], col) for x in (3, 2, 1)}
    factor([
        (1, [(XG[1, s], False) for s in range(2)] + [(second[s], False) for s in range(2)]
            + [(first[s], True) for s in range(2)] + [(CH[1, s], True) for s in range(2)]),
        (2, [(third[s], False) for s in range(2)] + [(CH[2, s], True) for s in range(2)]),
    ])
    for x in (1, 2, 3):
        step[x].wait_recv()
    FO[0] = ZG[1]
    FO[1] = ZG[2] + ZG[3]
    last = send(FO, FI, b_send.at[0], b_recv.at[0], core_mate, col)
    merge(0, [(0, 4), (0, 5)], [(1, 0), (1, 1)], [(1, 4), (1, 5)])
    merge(1, [(1, 4), (1, 5)], [(1, 2), (1, 3)], [(1, 6), (1, 7)])
    merge(2, [(1, 6), (1, 7)], [(2, 0), (2, 1)], [(2, 2), (2, 3)])
    last.wait_recv()
    swap = row % 2 == 1
    fourth = [jnp.where(swap, FI[0], FO[0]), jnp.where(swap, FO[0], FI[0])]
    fifth = [jnp.where(swap, FI[1], FO[1]), jnp.where(swap, FO[1], FI[1])]
    level = [CH[2, s] + fourth[s] for s in range(2)]
    factor([(3, [(v, False) for v in fourth + fifth] + [(v, True) for v in level] + [(level[s] + fifth[s], True) for s in range(2)])])
    merge(3, [(2, 2), (2, 3)], [(3, 0), (3, 1)], [(3, 4), (3, 5)])
    merge(4, [(3, 4), (3, 5)], [(3, 2), (3, 3)], [(3, 6), (3, 7)])
    for c in sent:
        c.wait_send()


def sketch(pattern, ranks, blocks, samples, probes, compress):
    vm = pl.BlockSpec(memory_space=pltpu.VMEM)
    sm = pl.BlockSpec(memory_space=pltpu.SMEM)
    hbm = pl.BlockSpec(memory_space=pltpu.HBM)
    dma = pltpu.SemaphoreType.DMA
    shape = jax.ShapeDtypeStruct
    return pl.pallas_call(
        sketch_kernel,
        out_shape=(
            shape((2, 2, 256, K), BF16), shape((2, 1, 5, 256, K), BF16),
        ),
        in_specs=[sm, sm, vm, hbm, hbm, hbm, hbm],
        out_specs=(vm, vm),
        scratch_shapes=[
            pltpu.VMEM((8, 256, 256), BF16),
            pltpu.VMEM((8, 5, 64, 256), BF16), pltpu.VMEM((8, 64, 256), BF16), pltpu.VMEM((256, K), F32), pltpu.VMEM((8, K), jnp.int32),
            pltpu.VMEM((2, 2, 8, 64, 256), BF16), pltpu.VMEM((2, 8, 64, 256), BF16),
            pltpu.VMEM((2, 8, K), jnp.int32), pltpu.SMEM((2, 8, K), jnp.int32),
            pltpu.VMEM((8, K, 256), F32), pltpu.VMEM((8, K, 256), F32),
            pltpu.VMEM((8, K, 256), F32), pltpu.VMEM((4, 2, K, 256), F32),
            pltpu.VMEM((8, 64, K), F32), pltpu.VMEM((2, 8, 64, K), F32), pltpu.VMEM((2, 8, 64, K), F32),
            pltpu.VMEM((4, 2, 64, K), F32), pltpu.VMEM((2, 256, K), F32),
            pltpu.VMEM((3, 2, K, K), F32), pltpu.VMEM((4, 2, K, K), F32), pltpu.VMEM((2, K, K), F32),
            pltpu.VMEM((4, K, K), F32), pltpu.VMEM((2, K, K), F32), pltpu.VMEM((2, K, K), F32),
            pltpu.VMEM((2, 2, 256, K), F32), pltpu.VMEM((2, 2, K, K), F32),
            pltpu.VMEM((4096, K), F32), pltpu.VMEM((4096, K), F32),
            dma((4,)), dma((2,)), dma((4,)), dma((4,)), dma((2, 4)), dma((2, 4)), dma((2, 4)), dma((2, 4)),
            dma((4,)), dma((4,)), dma((4,)), dma((4,)), dma((8,)), dma((8,)),
        ],
        compiler_params=pltpu.CompilerParams(
            collective_id=0, has_side_effects=True, vmem_limit_bytes=60 << 20
        ),
    )(pattern, ranks, pattern, blocks, samples, probes, compress)


def body(blocks, samples, probes, compress, pattern, ranks):
    return sketch(pattern, ranks, blocks, samples, probes, compress)


def solution(mesh):
    return jax.shard_map(
        body,
        mesh=mesh,
        in_specs=(
            P("row", None, "col", None),
            P("row", "col", None),
            P("row", "col", None),
            P(),
            P("row", None),
            P(),
        ),
        out_specs=(P(None, ("row", "col"), None, None), P(None, ("row", "col"), None, None, None)),
        check_vma=False,
    )
```
